1024 devices in a mesh: node: 32 (over y, x_lo), expert: 32 (over z, x_hi, core).
Axes of the slice: x: 8 (x_hi: 2, x_lo: 4; x = x_hi * 4 + x_lo), y: 8, z: 8, core: 2. Of those that a mesh axis runs over, the one named last changes fastest.
Arguments:
- grad_out: bfloat16 [8192, 7168], P(('node', 'expert')), may hold values from -6 to 6
- cross_rows: int32 [32, 32, 32, 1], P('node', 'expert'), may hold values from 0 to 7, as said below
- slot_rows: int32 [32, 32, 4, 16], P('node', 'expert'), may hold values from -1 to 31, as said below
- route_prob: float32 [32, 32, 4, 16], P('node', 'expert'), may hold values from 0.05 to 1
- w_down: bfloat16 [32, 32, 1024, 896], P('node', 'expert'), may hold values from -0.1875 to 0.1875
- gate_pre: bfloat16 [32, 32, 32, 16, 128], P('node', 'expert'), may hold values from -6 to 6
- up_pre: bfloat16 [32, 32, 32, 16, 128], P('node', 'expert'), may hold values from -6 to 6
Outputs:
- grad_gate: bfloat16 [32, 32, 32, 16, 128], P('node', 'expert')
- grad_up: bfloat16 [32, 32, 32, 16, 128], P('node', 'expert')
The draws below stay inside these ranges and needn't reach their ends.
Inputs may be any that keep to these rules, and one draw needn't show every extreme that they name: cross_rows[n, j, g, :] names distinct tokens of device (n, j) and has no empty place; every token of a device is named in exactly 4 of its device's 32 lists. The entries of slot_rows[g, j, e, :] that are not -1 are distinct and come before its -1 entries; they count from 4 to 16.
All inputs are finite; a program needn't handle non-finite values.
Results may differ from the reference program's by a relative error of at most 0.0049.
Values may be sent and summed in bfloat16 or wider, within the bound.
No kernel may reach another device: no remote copies, remote signals or barrier semaphores. Data moves between devices by JAX's collectives and lax.ppermute only.
A program may use at most 32 MiB of HBM per device.

```python
import math
import jax
import jax.numpy as jnp
from jax import lax

D = 7168
FF = 1024
SPLIT = 8
GROUPS_TOK = 4
TOK_DEV = 8
EXP_GROUP = 4
CAP_X = 1
ROWS_GW = 32
SLOTS = 16
COLS_DEV = 896
HID_DEV = 128
TOKENS = 8192
N_NODE = 32
N_EXPERT = 32


def draw_cross_rows(key, part):
    key = jax.random.fold_in(key, 11)
    device_keys = jax.random.split(key, N_NODE * N_EXPERT)
    stride = N_NODE // GROUPS_TOK

    def one_device(dev_key):
        order = jax.random.permutation(jax.random.fold_in(dev_key, 1), N_NODE).astype(jnp.int32)
        tokens = jnp.arange(TOK_DEV, dtype=jnp.int32)[:, None]
        spots = jnp.arange(N_NODE, dtype=jnp.int32)[None, :]
        member = jnp.zeros((TOK_DEV, N_NODE), jnp.int32)
        for index in range(GROUPS_TOK):
            member = member + ((tokens + index * stride) % N_NODE == spots).astype(jnp.int32)
        scores = jax.random.randint(jax.random.fold_in(dev_key, 2), (TOK_DEV, N_NODE), 0, 1 << 20) * TOK_DEV + tokens
        before = (scores[None, :, :] < scores[:, None, :]).astype(jnp.int32) * member[None, :, :]
        places = jnp.sum(before, axis=1)
        hits = member[:, :, None] * (places[:, :, None] == jnp.arange(CAP_X, dtype=jnp.int32)[None, None, :]).astype(jnp.int32)
        by_spot = jnp.sum(tokens[:, :, None] * hits, axis=0)
        return jnp.zeros((N_NODE, CAP_X), jnp.int32).at[order].set(by_spot)
    lists = jax.vmap(one_device)(device_keys)
    return lists.reshape(N_NODE, N_EXPERT, N_NODE, CAP_X).astype(jnp.int32)


def draw_slot_rows(key, part):
    key = jax.random.fold_in(key, 23)
    device_keys = jax.random.split(key, N_NODE * N_EXPERT)

    def one_device(dev_key):
        order = jax.random.permutation(jax.random.fold_in(dev_key, 1), ROWS_GW).astype(jnp.int32)
        experts_here = jnp.arange(EXP_GROUP, dtype=jnp.int32)[:, None]
        slot_index = jnp.arange(SLOTS, dtype=jnp.int32)[None, :]
        start = experts_here * ROWS_GW // EXP_GROUP
        taken = order[(start + slot_index) % ROWS_GW]
        kept = jax.random.randint(jax.random.fold_in(dev_key, 2), (EXP_GROUP, 1), SLOTS // 4, SLOTS + 1)
        return jnp.where(slot_index < kept, taken, -1).astype(jnp.int32)
    lists = jax.vmap(one_device)(device_keys)
    return lists.reshape(N_NODE, N_EXPERT, EXP_GROUP, SLOTS).astype(jnp.int32)


def level_of(own_key, extent, shards, least, high):
    def one(axis_at, shards_of):
        draws = jax.random.uniform(jax.random.fold_in(jax.random.fold_in(own_key, 6), axis_at), (shards_of,), jnp.float32, least / len(shards), high / len(shards))
        return jnp.repeat(jnp.exp(draws), extent[axis_at] // shards_of).reshape((-1,) + (1,) * (len(extent) - axis_at - 1))

    loudness = one(*shards[0])
    for cut in shards[1:]:
        loudness = loudness * one(*cut)
    return loudness


def normal_values(key, extent, deviation, most, cuts=(), kind=jnp.bfloat16):
    values = jax.random.normal(key, extent, jnp.float32) * deviation
    if len(cuts) > 0:
        values = level_of(key, extent, cuts, -0.22, 0.18) * values
    return jnp.clip(values, min=-most, max=most).astype(kind)


def setup_inputs(seed: int = 0) -> dict:
    splits = jax.random.split(jax.random.key(seed), 8)
    grad_out = normal_values(splits[0], (TOKENS, D), 1.0, 6.0, ((0, 1024),))
    cross_rows = draw_cross_rows(jax.random.fold_in(splits[7], 71), 0)
    slot_rows = draw_slot_rows(jax.random.fold_in(splits[7], 71), 0)
    route_prob = jnp.clip(jnp.exp(math.log(1.0) - 2.9957323 * jax.random.uniform(splits[3], (N_NODE, N_EXPERT, EXP_GROUP, SLOTS), jnp.float32) ** level_of(splits[3], (N_NODE, N_EXPERT, EXP_GROUP, SLOTS), ((0, 32), (1, 32)), -0.2, 0.2)), 0.05, 1.0)
    w_down = normal_values(splits[4], (N_NODE, N_EXPERT, FF, COLS_DEV), FF ** -0.5, 0.1875, ((0, 32), (1, 32)))
    gate_pre = normal_values(splits[5], (N_NODE, N_EXPERT, N_EXPERT, SLOTS, HID_DEV), 1.0, 6.0, ((0, 32), (1, 32)))
    up_pre = normal_values(splits[6], (N_NODE, N_EXPERT, N_EXPERT, SLOTS, HID_DEV), 1.0, 6.0, ((0, 32), (1, 32)))
    return {"grad_out": grad_out, "cross_rows": cross_rows, "slot_rows": slot_rows, "route_prob": route_prob, "w_down": w_down, "gate_pre": gate_pre, "up_pre": up_pre}


def reference(grad_out, cross_rows, slot_rows, route_prob, w_down, gate_pre, up_pre):
    cross_by_group = jnp.transpose(cross_rows, (2, 0, 1, 3))

    def per_group(items):
        token_lists, slot_list, weights_prob, weights, gate_saved, up_saved = items
        valid = slot_list >= 0
        placed = jnp.maximum(slot_list, 0).astype(jnp.int32)
        source = (placed // CAP_X).astype(jnp.int32)
        column = (placed % CAP_X).astype(jnp.int32)
        sender = jnp.arange(N_EXPERT, dtype=jnp.int32)[:, None, None]
        local = token_lists[source, sender, column].astype(jnp.int32)
        token = ((source * N_EXPERT + sender) * TOK_DEV + local).astype(jnp.int32)
        scaled = grad_out[token].astype(jnp.float32) * weights_prob[..., None]
        scaled = jnp.where(valid[..., None], scaled, jnp.zeros_like(scaled))
        dispatched = scaled.astype(jnp.bfloat16)
        full_cols = weights.reshape(EXP_GROUP, SPLIT, FF, COLS_DEV)
        full_cols = jnp.transpose(full_cols, (0, 2, 1, 3)).reshape(EXP_GROUP, FF, D)
        hidden_grad = jnp.einsum("jesd,efd->ejsf", dispatched.astype(jnp.float32), full_cols.astype(jnp.float32))
        hidden_grad = hidden_grad.reshape(EXP_GROUP, N_EXPERT, SLOTS, SPLIT, HID_DEV)
        hidden_grad = jnp.transpose(hidden_grad, (0, 3, 1, 2, 4)).reshape(N_EXPERT, N_EXPERT, SLOTS, HID_DEV)
        gate_vals = gate_saved.astype(jnp.float32)
        up_vals = up_saved.astype(jnp.float32)
        sigma = jax.nn.sigmoid(gate_vals)
        grad_up_rows = (hidden_grad * gate_vals * sigma).astype(jnp.bfloat16)
        grad_gate_rows = (hidden_grad * up_vals * sigma * (1.0 + gate_vals * (1.0 - sigma))).astype(jnp.bfloat16)
        return grad_gate_rows, grad_up_rows

    grad_gate, grad_up = lax.map(per_group, (cross_by_group, slot_rows, route_prob, w_down, gate_pre, up_pre))
    return grad_gate, grad_up
```

```python
import jax
import jax.numpy as jnp
from jax import lax
from jax.experimental import pallas as pl
from jax.experimental.pallas import tpu as pltpu
from jax.sharding import Mesh, PartitionSpec as P

NAMES = ("y", "xlo", "zhi", "zlo", "xhi", "core")
EXTENTS = (8, 4, 4, 2, 2, 2)
SWAP = ((0, 1), (1, 0))
STEPS = (0, 2, 1, 3)


def finish(place, keep, got, gate_factor, up_factor, grad_gate, grad_up):
    zhi, core = place[0], place[1]
    for piece, step in enumerate(STEPS):
        at = lax.rem(zhi + 4 - step, 4)
        for rows, whose in ((keep, core), (got, 1 - core)):
            value = rows[piece]
            grad_gate[at, :, whose] = (value * gate_factor[at, :, whose]).astype(grad_gate.dtype)
            grad_up[at, :, whose] = (value * up_factor[at, :, whose]).astype(grad_up.dtype)


def on_device(grad_out, cross_rows, slot_rows, route_prob, w_down, gate_pre, up_pre):
    bf16, f32 = jnp.bfloat16, jnp.float32
    tokens, width = grad_out.shape
    groups = cross_rows.shape[2]
    experts, slots = slot_rows.shape[2:]
    hidden, cols = w_down.shape[2:]
    block = gate_pre.shape[-1]
    core = lax.axis_index("core")

    w_own = w_down[0, 0]
    w_sib = lax.ppermute(w_own, "core", SWAP)

    tok = grad_out.reshape(tokens, 4, 2, cols)
    tok = jnp.where(core == 0, tok, tok[:, :, ::-1])
    picker = (
        cross_rows[0, 0, :, :] == jnp.arange(tokens, dtype=jnp.int32)[None, :]
    ).astype(bf16)
    outgoing = jnp.dot(
        picker, tok.reshape(tokens, width), preferred_element_type=f32
    ).astype(bf16)
    received = lax.all_to_all(
        outgoing.reshape(groups * 4, 2, cols),
        ("y", "xlo", "zlo", "xhi"),
        split_axis=0,
        concat_axis=0,
        tiled=True,
    ).reshape(groups, 4, 2 * cols)

    info = jnp.stack([slot_rows[0, 0].astype(f32), route_prob[0, 0]])
    info_z = lax.ppermute(info, "zlo", SWAP)
    zlo = lax.axis_index("zlo")
    info = jnp.where(zlo == 0, jnp.stack([info, info_z]), jnp.stack([info_z, info]))
    info_x = lax.ppermute(info, "xhi", SWAP)
    xhi = lax.axis_index("xhi")
    info = jnp.where(
        xhi == 0, jnp.stack([info, info_x], 1), jnp.stack([info_x, info], 1)
    ).reshape(4, 2, experts, slots)
    chosen = info[:, 0].astype(jnp.int32)
    prob = info[:, 1]
    chooser = (
        chosen[..., None] == jnp.arange(groups, dtype=jnp.int32)
    ).astype(bf16)
    selected = jnp.einsum("jesn,njd->ejsd", chooser, received, preferred_element_type=f32)
    scaled = (selected * jnp.transpose(prob, (1, 0, 2))[..., None]).astype(bf16)
    scaled = scaled.reshape(experts, 4 * slots, 2 * cols)

    zhi = lax.axis_index("zhi")
    pieces = [lax.dynamic_index_in_dim(scaled, zhi, 0, keepdims=False)]
    for step in STEPS[1:]:
        pairs = [(i, (i + step) % 4) for i in range(4)]
        out = lax.dynamic_index_in_dim(scaled, (zhi + step) % 4, 0, keepdims=False)
        pieces.append(lax.ppermute(out, "zhi", pairs))
    x = jnp.concatenate(pieces, 0)
    dims = (((1,), (1,)), ((), ()))
    half, quarter = hidden // 2, hidden // 4

    def product(start):
        own = lax.dynamic_slice_in_dim(w_own, start, half, 0)
        sib = lax.dynamic_slice_in_dim(w_sib, start, half, 0)
        value = lax.dot_general(x[:, :cols], own, dims, preferred_element_type=f32)
        return value + lax.dot_general(x[:, cols:], sib, dims, preferred_element_type=f32)

    give = product((1 - zlo) * half).astype(bf16)
    got = lax.ppermute(give, "zlo", SWAP)
    part = product(zlo * half) + got.astype(f32)
    give = lax.dynamic_slice_in_dim(part, (1 - xhi) * quarter, quarter, 1).astype(bf16)
    got = lax.ppermute(give, "xhi", SWAP)
    keep = lax.dynamic_slice_in_dim(part, xhi * quarter, quarter, 1)
    part = keep + got.astype(f32)
    give = lax.dynamic_slice_in_dim(part, (1 - core) * block, block, 1)
    keep = lax.dynamic_slice_in_dim(part, core * block, block, 1)
    got = lax.ppermute(give, "core", SWAP)

    gate_vals = gate_pre.astype(f32)
    up_vals = up_pre.astype(f32)
    sigma = jax.nn.sigmoid(gate_vals)
    up_factor = gate_vals * sigma
    gate_factor = up_vals * sigma * (1.0 + gate_vals * (1.0 - sigma))
    deep = (4, 4, 2, slots, block)
    place = jnp.stack([zhi, core]).astype(jnp.int32)
    grad_gate, grad_up = pl.pallas_call(
        finish,
        out_shape=[jax.ShapeDtypeStruct(deep, bf16)] * 2,
        in_specs=[pl.BlockSpec(memory_space=pltpu.SMEM)]
        + [pl.BlockSpec(memory_space=pltpu.VMEM)] * 4,
        out_specs=[pl.BlockSpec(memory_space=pltpu.VMEM)] * 2,
        compiler_params=pltpu.CompilerParams(vmem_limit_bytes=16 << 20),
    )(
        place,
        keep.reshape(4, 4, slots, block),
        got.reshape(4, 4, slots, block),
        gate_factor.reshape(deep),
        up_factor.reshape(deep),
    )
    return grad_gate.reshape(gate_pre.shape), grad_up.reshape(up_pre.shape)


def solution(mesh):
    fine = Mesh(mesh.devices.reshape(EXTENTS), NAMES)
    node, expert = NAMES[:2], NAMES[2:]
    flat = P(node, expert, None, None)
    deep = P(node, expert, None, None, None)
    return jax.shard_map(
        on_device,
        mesh=fine,
        in_specs=(P(node + expert, None), flat, flat, flat, flat, deep, deep),
        out_specs=(deep, deep),
        check_vma=False,
    )
```

```python
import jax
import jax.numpy as jnp
from jax import lax
from jax.experimental import pallas as pl
from jax.experimental.pallas import tpu as pltpu
from jax.sharding import Mesh, PartitionSpec as P

NAMES = ("y", "xlo", "zhi", "zlo", "xhi", "core")
EXTENTS = (8, 4, 4, 2, 2, 2)
SWAP = ((0, 1), (1, 0))
STEPS = (0, 2, 1, 3)
SMEM = pl.BlockSpec(memory_space=pltpu.SMEM)
VMEM = pl.BlockSpec(memory_space=pltpu.VMEM)


def pack(crossing_in, slots_in, weights_in, tokens_in, packed, *held):
    arrivals = held[4]
    sources = (crossing_in, slots_in, weights_in, tokens_in)
    copies = [
        pltpu.make_async_copy(source, held[index], arrivals.at[index])
        for index, source in enumerate(sources)
    ]
    for copy in copies:
        copy.start()
    for copy in copies:
        copy.wait()
    crossing, slot_rows, weights, tokens = held[:4]
    f32, bf16 = jnp.float32, jnp.bfloat16
    count, cols = tokens.shape[0], tokens.shape[1] // 8
    groups, span = crossing.shape[1], packed.shape[3]
    weight = weights[...]
    high = weight.astype(bf16).astype(f32)
    middle = (weight - high).astype(bf16).astype(f32)
    low = weight - high - middle
    parts = jnp.concatenate([slot_rows[...].astype(f32), high, middle, low], 0).astype(bf16)
    lines, slots = parts.shape
    behind = span - cols
    spread = (
        lax.broadcasted_iota(jnp.int32, (slots, behind), 1) % slots
        == lax.broadcasted_iota(jnp.int32, (slots, behind), 0)
    ).astype(bf16)
    spread = jnp.dot(parts, spread, preferred_element_type=f32)
    line = lax.broadcasted_iota(jnp.int32, (lines, behind), 0)
    place = lax.broadcasted_iota(jnp.int32, (lines, behind), 1) // slots
    table = [
        jnp.sum(
            jnp.where(line == place + side * lines // 2, spread, 0.0), axis=0, keepdims=True
        ).astype(bf16)
        for side in range(2)
    ]
    at = lax.broadcasted_iota(jnp.int32, (count, groups), 0)
    picker = (crossing[...] == at).astype(bf16)
    for pair in range(4):
        sides = []
        for side in range(2):
            start = (2 * pair + side) * cols
            value = lax.dot_general(
                picker,
                tokens[:, start : start + cols],
                (((0,), (0,)), ((), ())),
                preferred_element_type=f32,
            )
            behind_it = jnp.broadcast_to(table[side], (groups, behind))
            sides.append(jnp.concatenate([value.astype(bf16), behind_it], 1)[:, None, :])
        packed[:, pair, :, :] = jnp.concatenate(sides, 1)


def choose(place, rows, *outs_and_held):
    outs, held = outs_and_held[:4], outs_and_held[4]
    zhi, node = place[0], place[4]
    total, span = rows.shape[0], rows.shape[1] // 2
    cols = outs[0].shape[1] // 2
    slots = held.shape[1]
    wide = 4 * slots
    f32, bf16 = jnp.float32, jnp.bfloat16
    lane = lax.broadcasted_iota(jnp.int32, (8, total), 1)
    line = lax.broadcasted_iota(jnp.int32, (8, total), 0)
    own = (lane == node * 4 + line).astype(bf16)
    first = jnp.dot(own, rows[:, cols:span], preferred_element_type=f32)
    second = jnp.dot(own, rows[:, span + cols :], preferred_element_type=f32)
    at = lax.broadcasted_iota(jnp.int32, (total, wide), 0)
    dims = (((0,), (0,)), ((), ()))
    for gate in range(4):
        slot = first[gate : gate + 1, :wide].astype(jnp.int32)
        match = at == slot * 4 + gate
        weights = (first[gate : gate + 1, wide:], second[gate : gate + 1, :wide], second[gate : gate + 1, wide:])
        pickers = [jnp.where(match, part, 0.0).astype(bf16) for part in weights]
        for side in range(2):
            block = rows[:, side * span : side * span + cols]
            value = sum(
                lax.dot_general(p, block, dims, preferred_element_type=f32) for p in pickers
            ).astype(bf16)
            for expert in range(4):
                held[gate * 4 + expert, :, side * cols : (side + 1) * cols] = value[
                    expert * slots : (expert + 1) * slots
                ]
    for out, step in zip(outs, STEPS):
        expert = lax.rem(zhi + step, 4)
        for gate in range(4):
            out[gate * slots : (gate + 1) * slots, :] = held[gate * 4 + expert]


def arrange(place, w_own, w_sib, blocks):
    core, zlo, xhi = place[1], place[2], place[3]
    size, cols = blocks.shape[1], w_own.shape[1]
    own_at = pl.multiple_of(core * cols, 128)
    sib_at = pl.multiple_of((1 - core) * cols, 128)
    for index in range(4):
        z = 1 - zlo if index < 2 else zlo
        x = 1 - xhi if index % 2 == 0 else xhi
        rows = pl.ds(pl.multiple_of((z * 2 + x) * size, size), size)
        blocks[index, :, pl.ds(own_at, cols)] = w_own[rows, :]
        blocks[index, :, pl.ds(sib_at, cols)] = w_sib[rows, :]


def products(which, first, second, blocks, out):
    size = blocks.shape[1]
    both = jnp.concatenate([first[...], second[...]], 0)
    dims = (((1,), (1,)), ((), ()))
    for index, block in enumerate(which):
        value = lax.dot_general(both, blocks[block], dims, preferred_element_type=jnp.float32)
        out[:, index * size : (index + 1) * size] = value.astype(out.dtype)


def later_products(which, first, second, blocks, keep, got, out, kept):
    size = kept.shape[1]
    total = keep[...] + got[...].astype(jnp.float32)
    out[:, :size] = total[:, :size].astype(out.dtype)
    kept[...] = total[:, size:]
    products(which, first, second, blocks, out.at[:, size:])


def finish(place, keep, got, gate_factor, up_factor, grad_gate, grad_up):
    zhi, core = place[0], place[1]
    for piece, step in enumerate(STEPS):
        at = lax.rem(zhi + 4 - step, 4)
        for rows, whose in ((keep, core), (got, 1 - core)):
            value = rows[piece]
            grad_gate[at, :, whose] = (value * gate_factor[at, :, whose]).astype(grad_gate.dtype)
            grad_up[at, :, whose] = (value * up_factor[at, :, whose]).astype(grad_up.dtype)


def on_device(grad_out, cross_rows, slot_rows, route_prob, w_down, gate_pre, up_pre):
    bf16, f32 = jnp.bfloat16, jnp.float32
    groups = cross_rows.shape[2]
    experts, slots = slot_rows.shape[2:]
    hidden, cols = w_down.shape[2:]
    block = gate_pre.shape[-1]
    zhi, zlo = lax.axis_index("zhi"), lax.axis_index("zlo")
    xhi, core = lax.axis_index("xhi"), lax.axis_index("core")
    node = lax.axis_index("y") * EXTENTS[1] + lax.axis_index("xlo")
    w_own = w_down[0, 0]

    behind = 2 * experts * slots
    span = cols + behind
    inputs = (cross_rows.reshape(1, groups), slot_rows[0, 0], route_prob[0, 0], grad_out)
    outgoing = pl.pallas_call(
        pack,
        out_shape=jax.ShapeDtypeStruct((groups, 4, 2, span), bf16),
        in_specs=[pl.BlockSpec(memory_space=pl.ANY)] * 4,
        out_specs=VMEM,
        scratch_shapes=[pltpu.VMEM(v.shape, v.dtype) for v in inputs]
        + [pltpu.SemaphoreType.DMA((4,))],
        compiler_params=pltpu.CompilerParams(vmem_limit_bytes=56 << 20),
    )(*inputs)
    outgoing = outgoing.reshape(groups * 4, 2, span)
    place = jnp.stack([zhi, core, zlo, xhi, node]).astype(jnp.int32)
    received = lax.all_to_all(
        outgoing,
        ("y", "xlo", "zlo", "xhi"),
        split_axis=0,
        concat_axis=0,
        tiled=True,
    ).reshape(groups * 4, 2 * span)

    w_sib = lax.ppermute(w_own, "core", SWAP)
    size = (4 * slots, 2 * cols)
    chosen = pl.pallas_call(
        choose,
        out_shape=[jax.ShapeDtypeStruct(size, bf16)] * 4,
        in_specs=[SMEM, VMEM],
        out_specs=[VMEM] * 4,
        scratch_shapes=[pltpu.VMEM((4 * experts, slots, 2 * cols), bf16)],
        compiler_params=pltpu.CompilerParams(vmem_limit_bytes=12 << 20),
    )(place, received)
    pieces = [chosen[0]]
    for step, out in zip(STEPS[1:], chosen[1:]):
        pairs = [(i, (i + step) % 4) for i in range(4)]
        pieces.append(lax.ppermute(out, "zhi", pairs))
    rows = 2 * size[0]
    half, quarter = hidden // 2, hidden // 4

    blocks = pl.pallas_call(
        arrange,
        out_shape=jax.ShapeDtypeStruct((4, quarter, 2 * cols), bf16),
        in_specs=[SMEM] + [VMEM] * 2,
        out_specs=VMEM,
        compiler_params=pltpu.CompilerParams(vmem_limit_bytes=12 << 20),
    )(place, w_own, w_sib)

    def multiply(first, second, which, kind):
        return pl.pallas_call(
            lambda *refs: products(which, *refs),
            out_shape=jax.ShapeDtypeStruct((rows, half), kind),
            in_specs=[VMEM] * 3,
            out_specs=VMEM,
            compiler_params=pltpu.CompilerParams(vmem_limit_bytes=12 << 20),
            cost_estimate=pl.CostEstimate(
                flops=2 * rows * half * 2 * cols, bytes_accessed=3 << 20, transcendentals=0
            ),
        )(first, second, blocks)

    give = multiply(pieces[0], pieces[1], (0, 2), bf16)
    got = lax.ppermute(give, "xhi", SWAP)
    keep = multiply(pieces[0], pieces[1], (1, 3), f32)
    third, fourth, _, _ = lax.optimization_barrier((pieces[2], pieces[3], give, keep))
    give, keep_a = pl.pallas_call(
        lambda *refs: later_products((0, 1), *refs),
        out_shape=[
            jax.ShapeDtypeStruct((rows, quarter + half), bf16),
            jax.ShapeDtypeStruct((rows, quarter), f32),
        ],
        in_specs=[VMEM] * 5,
        out_specs=[VMEM] * 2,
        compiler_params=pltpu.CompilerParams(vmem_limit_bytes=12 << 20),
    )(third, fourth, blocks, keep, got)
    got = lax.ppermute(give, "zlo", SWAP)
    keep = multiply(third, fourth, (2, 3), f32)
    give = (keep[:, :quarter] + got[:, quarter:half].astype(f32)).astype(bf16)
    keep_b = keep[:, quarter:] + got[:, half:].astype(f32)
    keep_a = keep_a + got[:, :quarter].astype(f32)
    got = lax.ppermute(give, "xhi", SWAP)
    keep_b = keep_b + got.astype(f32)
    total = jnp.concatenate([keep_a, keep_b], 0)
    give = lax.dynamic_slice_in_dim(total, (1 - core) * block, block, 1)
    keep = lax.dynamic_slice_in_dim(total, core * block, block, 1)
    got = lax.ppermute(give, "core", SWAP)

    gate_vals = gate_pre.astype(f32)
    up_vals = up_pre.astype(f32)
    sigma = jax.nn.sigmoid(gate_vals)
    up_factor = gate_vals * sigma
    gate_factor = up_vals * sigma * (1.0 + gate_vals * (1.0 - sigma))
    deep = (4, 4, 2, slots, block)
    part = (4, 4, slots, block)
    grad_gate, grad_up = pl.pallas_call(
        finish,
        out_shape=[jax.ShapeDtypeStruct(deep, bf16)] * 2,
        in_specs=[SMEM] + [VMEM] * 4,
        out_specs=[VMEM] * 2,
        compiler_params=pltpu.CompilerParams(vmem_limit_bytes=8 << 20),
    )(
        place,
        keep.reshape(part),
        got.reshape(part),
        gate_factor.reshape(deep),
        up_factor.reshape(deep),
    )
    return grad_gate.reshape(gate_pre.shape), grad_up.reshape(up_pre.shape)


def solution(mesh):
    fine = Mesh(mesh.devices.reshape(EXTENTS), NAMES)
    node, expert = NAMES[:2], NAMES[2:]
    flat = P(node, expert, None, None)
    deep = P(node, expert, None, None, None)
    return jax.shard_map(
        on_device,
        mesh=fine,
        in_specs=(P(node + expert, None), flat, flat, flat, flat, deep, deep),
        out_specs=(deep, deep),
        check_vma=False,
    )
```

```python
import jax
import jax.numpy as jnp
from jax import lax
from jax.experimental import pallas as pl
from jax.experimental.pallas import tpu as pltpu
from jax.sharding import Mesh, PartitionSpec as P

NAMES = ("y", "xlo", "zhi", "zlo", "xhi", "core")
EXTENTS = (8, 4, 4, 2, 2, 2)
SWAP = ((0, 1), (1, 0))
STEPS = (0, 2, 1, 3)
SMEM = pl.BlockSpec(memory_space=pltpu.SMEM)
VMEM = pl.BlockSpec(memory_space=pltpu.VMEM)


def pack(crossing_in, slots_in, weights_in, tokens_in, packed, *held):
    arrivals = held[4]
    sources = (crossing_in, slots_in, weights_in, tokens_in)
    copies = [
        pltpu.make_async_copy(source, held[index], arrivals.at[index])
        for index, source in enumerate(sources)
    ]
    for copy in copies:
        copy.start()
    for copy in copies:
        copy.wait()
    crossing, slot_rows, weights, tokens = held[:4]
    f32, bf16 = jnp.float32, jnp.bfloat16
    count, cols = tokens.shape[0], tokens.shape[1] // 8
    groups, span = crossing.shape[1], packed.shape[3]
    weight = weights[...]
    high = weight.astype(bf16).astype(f32)
    middle = (weight - high).astype(bf16).astype(f32)
    low = weight - high - middle
    parts = jnp.concatenate([slot_rows[...].astype(f32), high, middle, low], 0).astype(bf16)
    lines, slots = parts.shape
    behind = span - cols
    spread = (
        lax.broadcasted_iota(jnp.int32, (slots, behind), 1) % slots
        == lax.broadcasted_iota(jnp.int32, (slots, behind), 0)
    ).astype(bf16)
    spread = jnp.dot(parts, spread, preferred_element_type=f32)
    line = lax.broadcasted_iota(jnp.int32, (lines, behind), 0)
    place = lax.broadcasted_iota(jnp.int32, (lines, behind), 1) // slots
    table = [
        jnp.sum(
            jnp.where(line == place + side * lines // 2, spread, 0.0), axis=0, keepdims=True
        ).astype(bf16)
        for side in range(2)
    ]
    at = lax.broadcasted_iota(jnp.int32, (count, groups), 0)
    picker = (crossing[...] == at).astype(bf16)
    for pair in range(4):
        sides = []
        for side in range(2):
            start = (2 * pair + side) * cols
            value = lax.dot_general(
                picker,
                tokens[:, start : start + cols],
                (((0,), (0,)), ((), ())),
                preferred_element_type=f32,
            )
            behind_it = jnp.broadcast_to(table[side], (groups, behind))
            sides.append(jnp.concatenate([value.astype(bf16), behind_it], 1)[:, None, :])
        packed[:, pair, :, :] = jnp.concatenate(sides, 1)


def choose(place, rows, *outs_and_scratch):
    outs, (held, tables) = outs_and_scratch[:4], outs_and_scratch[4:]
    zhi, node = place[0], place[4]
    total, span = rows.shape[0], rows.shape[1] // 2
    cols = outs[0].shape[1] // 2
    slots = held.shape[1]
    wide = 4 * slots
    f32, bf16 = jnp.float32, jnp.bfloat16
    lane = lax.broadcasted_iota(jnp.int32, (8, total), 1)
    line = lax.broadcasted_iota(jnp.int32, (8, total), 0)
    own = (lane == node * 4 + line).astype(bf16)
    first = jnp.dot(own, rows[:, cols:span], preferred_element_type=f32)
    second = jnp.dot(own, rows[:, span + cols :], preferred_element_type=f32)
    parts = (first[:, :wide], first[:, wide:], second[:, :wide], second[:, wide:])
    for gate in range(4):
        for part in range(4):
            tables[part : part + 1, gate * wide : (gate + 1) * wide] = parts[part][
                gate : gate + 1
            ]
    at = lax.broadcasted_iota(jnp.int32, (total, 4 * wide), 0)
    gate = lax.broadcasted_iota(jnp.int32, (1, 4 * wide), 1) // wide
    match = at == tables[0:1, :].astype(jnp.int32) * 4 + gate
    pickers = [
        jnp.where(match, tables[part : part + 1, :], 0.0).astype(bf16) for part in range(1, 4)
    ]
    dims = (((0,), (0,)), ((), ()))
    for side in range(2):
        block = rows[:, side * span : side * span + cols]
        value = sum(lax.dot_general(p, block, dims, preferred_element_type=f32) for p in pickers)
        held[:, :, side * cols : (side + 1) * cols] = value.astype(bf16).reshape(
            held.shape[0], slots, cols
        )
    for out, step in zip(outs, STEPS):
        expert = lax.rem(zhi + step, 4)
        for gate_at in range(4):
            out[gate_at * slots : (gate_at + 1) * slots, :] = held[gate_at * 4 + expert]


def arrange(place, w_own, w_sib, blocks):
    core, zlo, xhi = place[1], place[2], place[3]
    size, cols = blocks.shape[1], w_own.shape[1]
    own_at = pl.multiple_of(core * cols, 128)
    sib_at = pl.multiple_of((1 - core) * cols, 128)
    for index in range(4):
        z = 1 - zlo if index < 2 else zlo
        x = 1 - xhi if index % 2 == 0 else xhi
        rows = pl.ds(pl.multiple_of((z * 2 + x) * size, size), size)
        blocks[index, :, pl.ds(own_at, cols)] = w_own[rows, :]
        blocks[index, :, pl.ds(sib_at, cols)] = w_sib[rows, :]


def products(which, first, second, blocks, out):
    size = blocks.shape[1]
    both = jnp.concatenate([first[...], second[...]], 0)
    dims = (((1,), (1,)), ((), ()))
    for index, block in enumerate(which):
        value = lax.dot_general(both, blocks[block], dims, preferred_element_type=jnp.float32)
        out[:, index * size : (index + 1) * size] = value.astype(out.dtype)


def finish(place, keep, got, gate_factor, up_factor, grad_gate, grad_up):
    zhi, core = place[0], place[1]
    for piece, step in enumerate(STEPS):
        at = lax.rem(zhi + 4 - step, 4)
        for rows, whose in ((keep, core), (got, 1 - core)):
            value = rows[piece]
            grad_gate[at, :, whose] = (value * gate_factor[at, :, whose]).astype(grad_gate.dtype)
            grad_up[at, :, whose] = (value * up_factor[at, :, whose]).astype(grad_up.dtype)


def on_device(grad_out, cross_rows, slot_rows, route_prob, w_down, gate_pre, up_pre):
    bf16, f32 = jnp.bfloat16, jnp.float32
    groups = cross_rows.shape[2]
    experts, slots = slot_rows.shape[2:]
    hidden, cols = w_down.shape[2:]
    block = gate_pre.shape[-1]
    zhi, zlo = lax.axis_index("zhi"), lax.axis_index("zlo")
    xhi, core = lax.axis_index("xhi"), lax.axis_index("core")
    node = lax.axis_index("y") * EXTENTS[1] + lax.axis_index("xlo")
    w_own = w_down[0, 0]

    behind = 2 * experts * slots
    span = cols + behind
    inputs = (cross_rows.reshape(1, groups), slot_rows[0, 0], route_prob[0, 0], grad_out)
    outgoing = pl.pallas_call(
        pack,
        out_shape=jax.ShapeDtypeStruct((groups, 4, 2, span), bf16),
        in_specs=[pl.BlockSpec(memory_space=pl.ANY)] * 4,
        out_specs=VMEM,
        scratch_shapes=[pltpu.VMEM(v.shape, v.dtype) for v in inputs]
        + [pltpu.SemaphoreType.DMA((4,))],
        compiler_params=pltpu.CompilerParams(vmem_limit_bytes=56 << 20),
    )(*inputs)
    outgoing = outgoing.reshape(groups * 4, 2, span)
    place = jnp.stack([zhi, core, zlo, xhi, node]).astype(jnp.int32)
    received = lax.all_to_all(
        outgoing,
        ("y", "xlo", "zlo", "xhi"),
        split_axis=0,
        concat_axis=0,
        tiled=True,
    ).reshape(groups * 4, 2 * span)

    w_sib = lax.ppermute(w_own, "core", SWAP)
    size = (4 * slots, 2 * cols)
    chosen = pl.pallas_call(
        choose,
        out_shape=[jax.ShapeDtypeStruct(size, bf16)] * 4,
        in_specs=[SMEM, VMEM],
        out_specs=[VMEM] * 4,
        scratch_shapes=[
            pltpu.VMEM((4 * experts, slots, 2 * cols), bf16),
            pltpu.VMEM((4, 4 * experts * slots), f32),
        ],
        compiler_params=pltpu.CompilerParams(vmem_limit_bytes=12 << 20),
    )(place, received)
    pieces = [chosen[0]]
    for step, out in zip(STEPS[1:], chosen[1:]):
        pairs = [(i, (i + step) % 4) for i in range(4)]
        pieces.append(lax.ppermute(out, "zhi", pairs))
    rows = 2 * size[0]
    half, quarter = hidden // 2, hidden // 4

    blocks = pl.pallas_call(
        arrange,
        out_shape=jax.ShapeDtypeStruct((4, quarter, 2 * cols), bf16),
        in_specs=[SMEM] + [VMEM] * 2,
        out_specs=VMEM,
        compiler_params=pltpu.CompilerParams(vmem_limit_bytes=12 << 20),
    )(place, w_own, w_sib)

    def multiply(first, second, which, kind):
        return pl.pallas_call(
            lambda *refs: products(which, *refs),
            out_shape=jax.ShapeDtypeStruct((rows, half), kind),
            in_specs=[VMEM] * 3,
            out_specs=VMEM,
            compiler_params=pltpu.CompilerParams(vmem_limit_bytes=12 << 20),
            cost_estimate=pl.CostEstimate(
                flops=2 * rows * half * 2 * cols, bytes_accessed=3 << 20, transcendentals=0
            ),
        )(first, second, blocks)

    give_a = multiply(pieces[0], pieces[1], (0, 2), bf16)
    got_a = lax.ppermute(give_a, "xhi", SWAP)
    keep_a = multiply(pieces[0], pieces[1], (1, 3), f32)
    third, fourth, give_a, keep_a = lax.optimization_barrier(
        (pieces[2], pieces[3], give_a, keep_a)
    )
    give_b = multiply(third, fourth, (0, 1), bf16)
    got_b = lax.ppermute(give_b, "zlo", SWAP)
    give_a = (keep_a[:, :quarter] + got_a[:, :quarter].astype(f32)).astype(bf16)
    keep_a = keep_a[:, quarter:] + got_a[:, quarter:].astype(f32)
    third, give_a = lax.optimization_barrier((third, give_a))
    got_a = lax.ppermute(give_a, "zlo", SWAP)
    keep_b = multiply(third, fourth, (2, 3), f32)
    give_b = (keep_b[:, :quarter] + got_b[:, :quarter].astype(f32)).astype(bf16)
    keep_b = keep_b[:, quarter:] + got_b[:, quarter:].astype(f32)
    got_b = lax.ppermute(give_b, "xhi", SWAP)
    total = jnp.concatenate([keep_a + got_a.astype(f32), keep_b + got_b.astype(f32)], 0)
    give = lax.dynamic_slice_in_dim(total, (1 - core) * block, block, 1)
    keep = lax.dynamic_slice_in_dim(total, core * block, block, 1)
    got = lax.ppermute(give, "core", SWAP)

    gate_vals = gate_pre.astype(f32)
    up_vals = up_pre.astype(f32)
    sigma = jax.nn.sigmoid(gate_vals)
    up_factor = gate_vals * sigma
    gate_factor = up_vals * sigma * (1.0 + gate_vals * (1.0 - sigma))
    deep = (4, 4, 2, slots, block)
    part = (4, 4, slots, block)
    grad_gate, grad_up = pl.pallas_call(
        finish,
        out_shape=[jax.ShapeDtypeStruct(deep, bf16)] * 2,
        in_specs=[SMEM] + [VMEM] * 4,
        out_specs=[VMEM] * 2,
        compiler_params=pltpu.CompilerParams(vmem_limit_bytes=8 << 20),
    )(
        place,
        keep.reshape(part),
        got.reshape(part),
        gate_factor.reshape(deep),
        up_factor.reshape(deep),
    )
    return grad_gate.reshape(gate_pre.shape), grad_up.reshape(up_pre.shape)


def solution(mesh):
    fine = Mesh(mesh.devices.reshape(EXTENTS), NAMES)
    node, expert = NAMES[:2], NAMES[2:]
    flat = P(node, expert, None, None)
    deep = P(node, expert, None, None, None)
    return jax.shard_map(
        on_device,
        mesh=fine,
        in_specs=(P(node + expert, None), flat, flat, flat, flat, deep, deep),
        out_specs=(deep, deep),
        check_vma=False,
    )
```

```python
import jax
import jax.numpy as jnp
from jax import lax
from jax.experimental import pallas as pl
from jax.experimental.pallas import tpu as pltpu
from jax.sharding import Mesh, PartitionSpec as P

NAMES = ("y", "xlo", "zhi", "zlo", "xhi", "core")
EXTENTS = (8, 4, 4, 2, 2, 2)
SWAP = ((0, 1), (1, 0))
STEPS = (0, 2, 1, 3)
SMEM = pl.BlockSpec(memory_space=pltpu.SMEM)
VMEM = pl.BlockSpec(memory_space=pltpu.VMEM)


def pack(crossing_in, slots_in, weights_in, tokens_in, packed, *held):
    arrivals, built, leaving = held[4:]
    sources = (crossing_in, slots_in, weights_in, tokens_in)
    copies = [
        pltpu.make_async_copy(source, held[index], arrivals.at[index])
        for index, source in enumerate(sources)
    ]
    for copy in copies[::-1]:
        copy.start()
    for copy in copies[:3]:
        copy.wait()
    crossing, slot_rows, weights, tokens = held[:4]
    f32, bf16 = jnp.float32, jnp.bfloat16
    count, cols = tokens.shape[0], tokens.shape[1] // 8
    groups, span = crossing.shape[1], packed.shape[3]
    weight = weights[...]
    high = weight.astype(bf16).astype(f32)
    middle = (weight - high).astype(bf16).astype(f32)
    low = weight - high - middle
    parts = jnp.concatenate([slot_rows[...].astype(f32), high, middle, low], 0).astype(bf16)
    lines, slots = parts.shape
    behind = span - cols
    spread = (
        lax.broadcasted_iota(jnp.int32, (slots, behind), 1) % slots
        == lax.broadcasted_iota(jnp.int32, (slots, behind), 0)
    ).astype(bf16)
    spread = jnp.dot(parts, spread, preferred_element_type=f32)
    line = lax.broadcasted_iota(jnp.int32, (lines, behind), 0)
    place = lax.broadcasted_iota(jnp.int32, (lines, behind), 1) // slots
    table = [
        jnp.sum(
            jnp.where(line == place + side * lines // 2, spread, 0.0), axis=0, keepdims=True
        ).astype(bf16)
        for side in range(2)
    ]
    at = lax.broadcasted_iota(jnp.int32, (count, groups), 0)
    picker = (crossing[...] == at).astype(bf16)
    copies[3].wait()
    out_copies = []
    for pair in range(4):
        sides = []
        for side in range(2):
            start = (2 * pair + side) * cols
            value = lax.dot_general(
                picker,
                tokens[:, start : start + cols],
                (((0,), (0,)), ((), ())),
                preferred_element_type=f32,
            )
            behind_it = jnp.broadcast_to(table[side], (groups, behind))
            sides.append(jnp.concatenate([value.astype(bf16), behind_it], 1)[:, None, :])
        built[pair] = jnp.concatenate(sides, 1)
        copy = pltpu.make_async_copy(built.at[pair], packed.at[:, pair], leaving.at[pair])
        copy.start()
        out_copies.append(copy)
    for copy in out_copies:
        copy.wait()


def choose(place, rows, *outs_and_scratch):
    outs, (held, tables) = outs_and_scratch[:4], outs_and_scratch[4:]
    zhi, node = place[0], place[4]
    total, span = rows.shape[0], rows.shape[1] // 2
    cols = outs[0].shape[1] // 2
    slots = held.shape[1]
    wide = 4 * slots
    f32, bf16 = jnp.float32, jnp.bfloat16
    lane = lax.broadcasted_iota(jnp.int32, (8, total), 1)
    line = lax.broadcasted_iota(jnp.int32, (8, total), 0)
    own = (lane == node * 4 + line).astype(bf16)
    first = jnp.dot(own, rows[:, cols:span], preferred_element_type=f32)
    second = jnp.dot(own, rows[:, span + cols :], preferred_element_type=f32)
    parts = (first[:, :wide], first[:, wide:], second[:, :wide], second[:, wide:])
    for gate in range(4):
        for part in range(4):
            tables[part : part + 1, gate * wide : (gate + 1) * wide] = parts[part][
                gate : gate + 1
            ]
    at = lax.broadcasted_iota(jnp.int32, (total, 4 * wide), 0)
    gate = lax.broadcasted_iota(jnp.int32, (1, 4 * wide), 1) // wide
    match = at == tables[0:1, :].astype(jnp.int32) * 4 + gate
    pickers = [
        jnp.where(match, tables[part : part + 1, :], 0.0).astype(bf16) for part in range(1, 4)
    ]
    dims = (((0,), (0,)), ((), ()))
    for side in range(2):
        block = rows[:, side * span : side * span + cols]
        value = sum(lax.dot_general(p, block, dims, preferred_element_type=f32) for p in pickers)
        held[:, :, side * cols : (side + 1) * cols] = value.astype(bf16).reshape(
            held.shape[0], slots, cols
        )
    for out, step in zip(outs, STEPS):
        expert = lax.rem(zhi + step, 4)
        for gate_at in range(4):
            out[gate_at * slots : (gate_at + 1) * slots, :] = held[gate_at * 4 + expert]


def arrange(place, w_own, w_sib, blocks):
    core, zlo, xhi = place[1], place[2], place[3]
    size, cols = blocks.shape[1], w_own.shape[1]
    own_at = pl.multiple_of(core * cols, 128)
    sib_at = pl.multiple_of((1 - core) * cols, 128)
    for index in range(4):
        z = 1 - zlo if index < 2 else zlo
        x = 1 - xhi if index % 2 == 0 else xhi
        rows = pl.ds(pl.multiple_of((z * 2 + x) * size, size), size)
        blocks[index, :, pl.ds(own_at, cols)] = w_own[rows, :]
        blocks[index, :, pl.ds(sib_at, cols)] = w_sib[rows, :]


def products(which, first, second, blocks, out):
    size = blocks.shape[1]
    both = jnp.concatenate([first[...], second[...]], 0)
    dims = (((1,), (1,)), ((), ()))
    for index, block in enumerate(which):
        value = lax.dot_general(both, blocks[block], dims, preferred_element_type=jnp.float32)
        out[:, index * size : (index + 1) * size] = value.astype(out.dtype)


def finish(place, keep, got, gate_factor, up_factor, grad_gate, grad_up):
    zhi, core = place[0], place[1]
    for piece, step in enumerate(STEPS):
        at = lax.rem(zhi + 4 - step, 4)
        for rows, whose in ((keep, core), (got, 1 - core)):
            value = rows[piece]
            grad_gate[at, :, whose] = (value * gate_factor[at, :, whose]).astype(grad_gate.dtype)
            grad_up[at, :, whose] = (value * up_factor[at, :, whose]).astype(grad_up.dtype)


def on_device(grad_out, cross_rows, slot_rows, route_prob, w_down, gate_pre, up_pre):
    bf16, f32 = jnp.bfloat16, jnp.float32
    groups = cross_rows.shape[2]
    experts, slots = slot_rows.shape[2:]
    hidden, cols = w_down.shape[2:]
    block = gate_pre.shape[-1]
    zhi, zlo = lax.axis_index("zhi"), lax.axis_index("zlo")
    xhi, core = lax.axis_index("xhi"), lax.axis_index("core")
    node = lax.axis_index("y") * EXTENTS[1] + lax.axis_index("xlo")
    w_own = w_down[0, 0]

    behind = 2 * experts * slots
    span = cols + behind
    inputs = (cross_rows.reshape(1, groups), slot_rows[0, 0], route_prob[0, 0], grad_out)
    outgoing = pl.pallas_call(
        pack,
        out_shape=jax.ShapeDtypeStruct((groups, 4, 2, span), bf16),
        in_specs=[pl.BlockSpec(memory_space=pl.ANY)] * 4,
        out_specs=pl.BlockSpec(memory_space=pl.ANY),
        scratch_shapes=[pltpu.VMEM(v.shape, v.dtype) for v in inputs]
        + [
            pltpu.SemaphoreType.DMA((4,)),
            pltpu.VMEM((4, groups, 2, span), bf16),
            pltpu.SemaphoreType.DMA((4,)),
        ],
        compiler_params=pltpu.CompilerParams(vmem_limit_bytes=56 << 20),
    )(*inputs)
    outgoing = outgoing.reshape(groups * 4, 2, span)
    place = jnp.stack([zhi, core, zlo, xhi, node]).astype(jnp.int32)
    received = lax.all_to_all(
        outgoing,
        ("y", "xlo", "zlo", "xhi"),
        split_axis=0,
        concat_axis=0,
        tiled=True,
    ).reshape(groups * 4, 2 * span)

    w_sib = lax.ppermute(w_own, "core", SWAP)
    size = (4 * slots, 2 * cols)
    chosen = pl.pallas_call(
        choose,
        out_shape=[jax.ShapeDtypeStruct(size, bf16)] * 4,
        in_specs=[SMEM, VMEM],
        out_specs=[VMEM] * 4,
        scratch_shapes=[
            pltpu.VMEM((4 * experts, slots, 2 * cols), bf16),
            pltpu.VMEM((4, 4 * experts * slots), f32),
        ],
        compiler_params=pltpu.CompilerParams(vmem_limit_bytes=12 << 20),
        cost_estimate=pl.CostEstimate(flops=20 << 30, bytes_accessed=2 << 20, transcendentals=0),
    )(place, received)
    pieces = [chosen[0]]
    for step, out in zip(STEPS[1:], chosen[1:]):
        pairs = [(i, (i + step) % 4) for i in range(4)]
        pieces.append(lax.ppermute(out, "zhi", pairs))
    rows = 2 * size[0]
    half, quarter = hidden // 2, hidden // 4

    blocks = pl.pallas_call(
        arrange,
        out_shape=jax.ShapeDtypeStruct((4, quarter, 2 * cols), bf16),
        in_specs=[SMEM] + [VMEM] * 2,
        out_specs=VMEM,
        compiler_params=pltpu.CompilerParams(vmem_limit_bytes=12 << 20),
    )(place, w_own, w_sib)

    def multiply(first, second, which, kind):
        return pl.pallas_call(
            lambda *refs: products(which, *refs),
            out_shape=jax.ShapeDtypeStruct((rows, half), kind),
            in_specs=[VMEM] * 3,
            out_specs=VMEM,
            compiler_params=pltpu.CompilerParams(vmem_limit_bytes=12 << 20),
            cost_estimate=pl.CostEstimate(
                flops=2 * rows * half * 2 * cols, bytes_accessed=3 << 20, transcendentals=0
            ),
        )(first, second, blocks)

    give_a = multiply(pieces[0], pieces[1], (0, 2), bf16)
    got_a = lax.ppermute(give_a, "xhi", SWAP)
    third, fourth, give_a = lax.optimization_barrier((pieces[2], pieces[3], give_a))
    give_b = multiply(third, fourth, (0, 1), bf16)
    first, give_b = lax.optimization_barrier((pieces[0], give_b))
    keep_a = multiply(first, pieces[1], (1, 3), f32)
    got_b = lax.ppermute(give_b, "zlo", SWAP)
    give_a = (keep_a[:, :quarter] + got_a[:, :quarter].astype(f32)).astype(bf16)
    keep_a = keep_a[:, quarter:] + got_a[:, quarter:].astype(f32)
    third, give_a = lax.optimization_barrier((third, give_a))
    got_a = lax.ppermute(give_a, "zlo", SWAP)
    keep_b = multiply(third, fourth, (2, 3), f32)
    give_b = (keep_b[:, :quarter] + got_b[:, :quarter].astype(f32)).astype(bf16)
    keep_b = keep_b[:, quarter:] + got_b[:, quarter:].astype(f32)
    got_b = lax.ppermute(give_b, "xhi", SWAP)
    total = jnp.concatenate([keep_a + got_a.astype(f32), keep_b + got_b.astype(f32)], 0)
    give = lax.dynamic_slice_in_dim(total, (1 - core) * block, block, 1)
    keep = lax.dynamic_slice_in_dim(total, core * block, block, 1)
    got = lax.ppermute(give, "core", SWAP)

    gate_vals = gate_pre.astype(f32)
    up_vals = up_pre.astype(f32)
    sigma = jax.nn.sigmoid(gate_vals)
    up_factor = gate_vals * sigma
    gate_factor = up_vals * sigma * (1.0 + gate_vals * (1.0 - sigma))
    deep = (4, 4, 2, slots, block)
    part = (4, 4, slots, block)
    grad_gate, grad_up = pl.pallas_call(
        finish,
        out_shape=[jax.ShapeDtypeStruct(deep, bf16)] * 2,
        in_specs=[SMEM] + [VMEM] * 4,
        out_specs=[VMEM] * 2,
        compiler_params=pltpu.CompilerParams(vmem_limit_bytes=8 << 20),
    )(
        place,
        keep.reshape(part),
        got.reshape(part),
        gate_factor.reshape(deep),
        up_factor.reshape(deep),
    )
    return grad_gate.reshape(gate_pre.shape), grad_up.reshape(up_pre.shape)


def solution(mesh):
    fine = Mesh(mesh.devices.reshape(EXTENTS), NAMES)
    node, expert = NAMES[:2], NAMES[2:]
    flat = P(node, expert, None, None)
    deep = P(node, expert, None, None, None)
    return jax.shard_map(
        on_device,
        mesh=fine,
        in_specs=(P(node + expert, None), flat, flat, flat, flat, deep, deep),
        out_specs=(deep, deep),
        check_vma=False,
    )
```

```python
import jax
import jax.numpy as jnp
from jax import lax
from jax.experimental import pallas as pl
from jax.experimental.pallas import tpu as pltpu
from jax.sharding import Mesh, PartitionSpec as P

NAMES = ("y", "xlo", "zhi", "zlo", "xhi", "core")
EXTENTS = (8, 4, 4, 2, 2, 2)
SWAP = ((0, 1), (1, 0))
STEPS = (0, 2, 1, 3)
SMEM = pl.BlockSpec(memory_space=pltpu.SMEM)
VMEM = pl.BlockSpec(memory_space=pltpu.VMEM)


def pack(crossing_in, slots_in, weights_in, tokens_in, packed, *held):
    arrivals, built, leaving = held[4:]
    sources = (crossing_in, slots_in, weights_in, tokens_in)
    copies = [
        pltpu.make_async_copy(source, held[index], arrivals.at[index])
        for index, source in enumerate(sources)
    ]
    for copy in copies[::-1]:
        copy.start()
    for copy in copies[:3]:
        copy.wait()
    crossing, slot_rows, weights, tokens = held[:4]
    f32, bf16 = jnp.float32, jnp.bfloat16
    count, cols = tokens.shape[0], tokens.shape[1] // 8
    groups, span = crossing.shape[1], packed.shape[3]
    weight = weights[...]
    high = weight.astype(bf16).astype(f32)
    middle = (weight - high).astype(bf16).astype(f32)
    low = weight - high - middle
    parts = jnp.concatenate([slot_rows[...].astype(f32), high, middle, low], 0).astype(bf16)
    lines, slots = parts.shape
    behind = span - cols
    spread = (
        lax.broadcasted_iota(jnp.int32, (slots, behind), 1) % slots
        == lax.broadcasted_iota(jnp.int32, (slots, behind), 0)
    ).astype(bf16)
    spread = jnp.dot(parts, spread, preferred_element_type=f32)
    line = lax.broadcasted_iota(jnp.int32, (lines, behind), 0)
    place = lax.broadcasted_iota(jnp.int32, (lines, behind), 1) // slots
    table = [
        jnp.sum(
            jnp.where(line == place + side * lines // 2, spread, 0.0), axis=0, keepdims=True
        ).astype(bf16)
        for side in range(2)
    ]
    at = lax.broadcasted_iota(jnp.int32, (count, groups), 0)
    picker = (crossing[...] == at).astype(bf16)
    copies[3].wait()
    out_copies = []
    for pair in range(4):
        sides = []
        for side in range(2):
            start = (2 * pair + side) * cols
            value = lax.dot_general(
                picker,
                tokens[:, start : start + cols],
                (((0,), (0,)), ((), ())),
                preferred_element_type=f32,
            )
            behind_it = jnp.broadcast_to(table[side], (groups, behind))
            sides.append(jnp.concatenate([value.astype(bf16), behind_it], 1)[:, None, :])
        built[pair] = jnp.concatenate(sides, 1)
        copy = pltpu.make_async_copy(built.at[pair], packed.at[:, pair], leaving.at[pair])
        copy.start()
        out_copies.append(copy)
    for copy in out_copies:
        copy.wait()


def choose(place, rows, *outs_and_scratch):
    outs, tables = outs_and_scratch[:4], outs_and_scratch[4]
    zhi, node = place[0], place[4]
    total, span = rows.shape[0], rows.shape[1] // 2
    cols = outs[0].shape[1] // 2
    wide = outs[0].shape[0]
    slots = wide // 4
    f32, bf16, i32 = jnp.float32, jnp.bfloat16, jnp.int32
    lane = lax.broadcasted_iota(i32, (8, total), 1)
    line = lax.broadcasted_iota(i32, (8, total), 0)
    own = (lane == node * 4 + line).astype(bf16)
    first = jnp.dot(own, rows[:, cols:span], preferred_element_type=f32)
    second = jnp.dot(own, rows[:, span + cols :], preferred_element_type=f32)
    parts = (first[:, :wide], first[:, wide:], second[:, :wide], second[:, wide:])
    for gate in range(4):
        for part in range(4):
            tables[part : part + 1, gate * wide : (gate + 1) * wide] = parts[part][
                gate : gate + 1
            ]
    to = lax.broadcasted_iota(i32, (1, 4 * wide), 1)
    step = jnp.zeros((1, 4 * wide), i32)
    for index, value in enumerate(STEPS):
        step = jnp.where(to // wide == index, value, step)
    gate = (to % wide) // slots
    source = gate * wide + ((zhi + step) % 4) * slots + to % slots
    move = (lax.broadcasted_iota(i32, (4 * wide, 4 * wide), 0) == source).astype(bf16)
    table = jnp.dot(tables[...].astype(bf16), move, preferred_element_type=f32)
    at = lax.broadcasted_iota(i32, (total, 4 * wide), 0)
    match = at == table[0:1, :].astype(i32) * 4 + gate
    pickers = [
        jnp.where(match, table[part : part + 1, :], 0.0).astype(bf16) for part in range(1, 4)
    ]
    dims = (((0,), (0,)), ((), ()))
    for side in range(2):
        block = rows[:, side * span : side * span + cols]
        value = sum(lax.dot_general(p, block, dims, preferred_element_type=f32) for p in pickers)
        value = value.astype(bf16)
        for index, out in enumerate(outs):
            out[:, side * cols : (side + 1) * cols] = value[index * wide : (index + 1) * wide]


def arrange(place, w_own, w_sib, blocks):
    core, zlo, xhi = place[1], place[2], place[3]
    size, cols = blocks.shape[1], w_own.shape[1]
    own_at = pl.multiple_of(core * cols, 128)
    sib_at = pl.multiple_of((1 - core) * cols, 128)
    for index in range(4):
        z = 1 - zlo if index < 2 else zlo
        x = 1 - xhi if index % 2 == 0 else xhi
        rows = pl.ds(pl.multiple_of((z * 2 + x) * size, size), size)
        blocks[index, :, pl.ds(own_at, cols)] = w_own[rows, :]
        blocks[index, :, pl.ds(sib_at, cols)] = w_sib[rows, :]


def products(which, first, second, blocks, out):
    size = blocks.shape[1]
    both = jnp.concatenate([first[...], second[...]], 0)
    dims = (((1,), (1,)), ((), ()))
    for index, block in enumerate(which):
        value = lax.dot_general(both, blocks[block], dims, preferred_element_type=jnp.float32)
        out[:, index * size : (index + 1) * size] = value.astype(out.dtype)


def finish(place, keep, got, gate_factor, up_factor, grad_gate, grad_up, built, leaving):
    zhi, core = place[0], place[1]
    copies = []
    for piece, step in enumerate(STEPS):
        at = lax.rem(zhi + 4 - step, 4)
        for rows, whose in ((keep, core), (got, 1 - core)):
            value = rows[piece]
            built[0, piece, :, whose] = (value * gate_factor[at, :, whose]).astype(built.dtype)
            built[1, piece, :, whose] = (value * up_factor[at, :, whose]).astype(built.dtype)
        for index, out in enumerate((grad_gate, grad_up)):
            copy = pltpu.make_async_copy(
                built.at[index, piece], out.at[at], leaving.at[index, piece]
            )
            copy.start()
            copies.append(copy)
    for copy in copies:
        copy.wait()


def on_device(grad_out, cross_rows, slot_rows, route_prob, w_down, gate_pre, up_pre):
    bf16, f32 = jnp.bfloat16, jnp.float32
    groups = cross_rows.shape[2]
    experts, slots = slot_rows.shape[2:]
    hidden, cols = w_down.shape[2:]
    block = gate_pre.shape[-1]
    zhi, zlo = lax.axis_index("zhi"), lax.axis_index("zlo")
    xhi, core = lax.axis_index("xhi"), lax.axis_index("core")
    node = lax.axis_index("y") * EXTENTS[1] + lax.axis_index("xlo")
    w_own = w_down[0, 0]

    behind = 2 * experts * slots
    span = cols + behind
    inputs = (cross_rows.reshape(1, groups), slot_rows[0, 0], route_prob[0, 0], grad_out)
    outgoing = pl.pallas_call(
        pack,
        out_shape=jax.ShapeDtypeStruct((groups, 4, 2, span), bf16),
        in_specs=[pl.BlockSpec(memory_space=pl.ANY)] * 4,
        out_specs=pl.BlockSpec(memory_space=pl.ANY),
        scratch_shapes=[pltpu.VMEM(v.shape, v.dtype) for v in inputs]
        + [
            pltpu.SemaphoreType.DMA((4,)),
            pltpu.VMEM((4, groups, 2, span), bf16),
            pltpu.SemaphoreType.DMA((4,)),
        ],
        compiler_params=pltpu.CompilerParams(vmem_limit_bytes=56 << 20),
    )(*inputs)
    outgoing = outgoing.reshape(groups * 4, 2, span)
    place = jnp.stack([zhi, core, zlo, xhi, node]).astype(jnp.int32)
    received = lax.all_to_all(
        outgoing,
        ("y", "xlo", "zlo", "xhi"),
        split_axis=0,
        concat_axis=0,
        tiled=True,
    ).reshape(groups * 4, 2 * span)

    w_sib = lax.ppermute(w_own, "core", SWAP)
    size = (4 * slots, 2 * cols)
    chosen = pl.pallas_call(
        choose,
        out_shape=[jax.ShapeDtypeStruct(size, bf16)] * 4,
        in_specs=[SMEM, VMEM],
        out_specs=[VMEM] * 4,
        scratch_shapes=[
            pltpu.VMEM((4, 4 * experts * slots), f32),
        ],
        compiler_params=pltpu.CompilerParams(vmem_limit_bytes=12 << 20),
        cost_estimate=pl.CostEstimate(flops=20 << 30, bytes_accessed=2 << 20, transcendentals=0),
    )(place, received)
    pieces = [chosen[0]]
    for step, out in zip(STEPS[1:], chosen[1:]):
        pairs = [(i, (i + step) % 4) for i in range(4)]
        pieces.append(lax.ppermute(out, "zhi", pairs))
    rows = 2 * size[0]
    half, quarter = hidden // 2, hidden // 4

    blocks = pl.pallas_call(
        arrange,
        out_shape=jax.ShapeDtypeStruct((4, quarter, 2 * cols), bf16),
        in_specs=[SMEM] + [VMEM] * 2,
        out_specs=VMEM,
        compiler_params=pltpu.CompilerParams(vmem_limit_bytes=12 << 20),
    )(place, w_own, w_sib)

    def multiply(first, second, which, kind):
        return pl.pallas_call(
            lambda *refs: products(which, *refs),
            out_shape=jax.ShapeDtypeStruct((rows, half), kind),
            in_specs=[VMEM] * 3,
            out_specs=VMEM,
            compiler_params=pltpu.CompilerParams(vmem_limit_bytes=12 << 20),
            cost_estimate=pl.CostEstimate(
                flops=2 * rows * half * 2 * cols, bytes_accessed=3 << 20, transcendentals=0
            ),
        )(first, second, blocks)

    give_a = multiply(pieces[0], pieces[1], (0, 2), bf16)
    got_a = lax.ppermute(give_a, "xhi", SWAP)
    third, fourth, give_a = lax.optimization_barrier((pieces[2], pieces[3], give_a))
    give_b = multiply(third, fourth, (0, 1), bf16)
    first, give_b = lax.optimization_barrier((pieces[0], give_b))
    keep_a = multiply(first, pieces[1], (1, 3), f32)
    got_b = lax.ppermute(give_b, "zlo", SWAP)
    give_a = (keep_a[:, :quarter] + got_a[:, :quarter].astype(f32)).astype(bf16)
    keep_a = keep_a[:, quarter:] + got_a[:, quarter:].astype(f32)
    third, give_a = lax.optimization_barrier((third, give_a))
    got_a = lax.ppermute(give_a, "zlo", SWAP)
    keep_b = multiply(third, fourth, (2, 3), f32)
    give_b = (keep_b[:, :quarter] + got_b[:, :quarter].astype(f32)).astype(bf16)
    keep_b = keep_b[:, quarter:] + got_b[:, quarter:].astype(f32)
    got_b = lax.ppermute(give_b, "xhi", SWAP)
    total = jnp.concatenate([keep_a + got_a.astype(f32), keep_b + got_b.astype(f32)], 0)
    give = lax.dynamic_slice_in_dim(total, (1 - core) * block, block, 1)
    keep = lax.dynamic_slice_in_dim(total, core * block, block, 1)
    got = lax.ppermute(give, "core", SWAP)

    gate_vals = gate_pre.astype(f32)
    up_vals = up_pre.astype(f32)
    sigma = jax.nn.sigmoid(gate_vals)
    up_factor = gate_vals * sigma
    gate_factor = up_vals * sigma * (1.0 + gate_vals * (1.0 - sigma))
    deep = (4, 4, 2, slots, block)
    part = (4, 4, slots, block)
    grad_gate, grad_up = pl.pallas_call(
        finish,
        out_shape=[jax.ShapeDtypeStruct(deep, bf16)] * 2,
        in_specs=[SMEM] + [VMEM] * 4,
        out_specs=[pl.BlockSpec(memory_space=pl.ANY)] * 2,
        scratch_shapes=[pltpu.VMEM((2,) + deep, bf16), pltpu.SemaphoreType.DMA((2, 4))],
        compiler_params=pltpu.CompilerParams(vmem_limit_bytes=8 << 20),
    )(
        place,
        keep.reshape(part),
        got.reshape(part),
        gate_factor.reshape(deep),
        up_factor.reshape(deep),
    )
    return grad_gate.reshape(gate_pre.shape), grad_up.reshape(up_pre.shape)


def solution(mesh):
    fine = Mesh(mesh.devices.reshape(EXTENTS), NAMES)
    node, expert = NAMES[:2], NAMES[2:]
    flat = P(node, expert, None, None)
    deep = P(node, expert, None, None, None)
    return jax.shard_map(
        on_device,
        mesh=fine,
        in_specs=(P(node + expert, None), flat, flat, flat, flat, deep, deep),
        out_specs=(deep, deep),
        check_vma=False,
    )
```

```python
import jax
import jax.numpy as jnp
from jax import lax
from jax.experimental import pallas as pl
from jax.experimental.pallas import tpu as pltpu
from jax.sharding import Mesh, PartitionSpec as P

NAMES = ("y", "xlo", "zhi", "zlo", "xhi", "core")
EXTENTS = (8, 4, 4, 2, 2, 2)
SWAP = ((0, 1), (1, 0))
STEPS = (0, 2, 1, 3)
SMEM = pl.BlockSpec(memory_space=pltpu.SMEM)
VMEM = pl.BlockSpec(memory_space=pltpu.VMEM)


def pack(crossing_in, slots_in, weights_in, tokens_in, packed, *held):
    arrivals, built, leaving = held[4:]
    sources = (crossing_in, slots_in, weights_in, tokens_in)
    copies = [
        pltpu.make_async_copy(source, held[index], arrivals.at[index])
        for index, source in enumerate(sources)
    ]
    for copy in copies[::-1]:
        copy.start()
    for copy in copies[:3]:
        copy.wait()
    crossing, slot_rows, weights, tokens = held[:4]
    f32, bf16 = jnp.float32, jnp.bfloat16
    count, cols = tokens.shape[0], tokens.shape[1] // 8
    groups, span = crossing.shape[1], packed.shape[3]
    weight = weights[...]
    high = weight.astype(bf16).astype(f32)
    middle = (weight - high).astype(bf16).astype(f32)
    low = weight - high - middle
    parts = jnp.concatenate([slot_rows[...].astype(f32), high, middle, low], 0).astype(bf16)
    lines, slots = parts.shape
    behind = span - cols
    spread = (
        lax.broadcasted_iota(jnp.int32, (slots, behind), 1) % slots
        == lax.broadcasted_iota(jnp.int32, (slots, behind), 0)
    ).astype(bf16)
    spread = jnp.dot(parts, spread, preferred_element_type=f32)
    line = lax.broadcasted_iota(jnp.int32, (lines, behind), 0)
    place = lax.broadcasted_iota(jnp.int32, (lines, behind), 1) // slots
    table = [
        jnp.sum(
            jnp.where(line == place + side * lines // 2, spread, 0.0), axis=0, keepdims=True
        ).astype(bf16)
        for side in range(2)
    ]
    half = lax.broadcasted_iota(jnp.int32, (groups, 2 * groups), 1) // 2
    twice = (half == lax.broadcasted_iota(jnp.int32, (groups, 2 * groups), 0)).astype(bf16)
    token = jnp.dot(crossing[...].astype(bf16), twice, preferred_element_type=f32)
    side = lax.broadcasted_iota(jnp.int32, (1, 2 * groups), 1) % 2
    at = lax.broadcasted_iota(jnp.int32, (2 * count, 2 * groups), 0)
    picker = (at == side * count + token.astype(jnp.int32)).astype(bf16)
    odd = lax.broadcasted_iota(jnp.int32, (2 * groups, behind), 0) % 2 == 1
    tail = jnp.where(odd, table[1].astype(f32), table[0].astype(f32)).astype(bf16)
    copies[3].wait()
    out_copies = []
    for pair in range(4):
        start = 2 * pair * cols
        both = jnp.concatenate(
            [tokens[:, start : start + cols], tokens[:, start + cols : start + 2 * cols]], 0
        )
        value = lax.dot_general(
            picker, both, (((0,), (0,)), ((), ())), preferred_element_type=f32
        )
        rows = jnp.concatenate([value.astype(bf16), tail], 1)
        built[pair] = rows.reshape(groups, 2, cols + behind)
        copy = pltpu.make_async_copy(built.at[pair], packed.at[:, pair], leaving.at[pair])
        copy.start()
        out_copies.append(copy)
    for copy in out_copies:
        copy.wait()


def choose(place, rows, *outs_and_scratch):
    outs, (held, tables) = outs_and_scratch[:4], outs_and_scratch[4:]
    zhi, node = place[0], place[4]
    total, span = rows.shape[0], rows.shape[1] // 2
    cols = outs[0].shape[1] // 2
    slots = held.shape[1]
    wide = 4 * slots
    f32, bf16 = jnp.float32, jnp.bfloat16
    lane = lax.broadcasted_iota(jnp.int32, (8, total), 1)
    line = lax.broadcasted_iota(jnp.int32, (8, total), 0)
    own = (lane == node * 4 + line).astype(bf16)
    first = jnp.dot(own, rows[:, cols:span], preferred_element_type=f32)
    second = jnp.dot(own, rows[:, span + cols :], preferred_element_type=f32)
    parts = (first[:, :wide], first[:, wide:], second[:, :wide], second[:, wide:])
    for gate in range(4):
        for part in range(4):
            tables[part : part + 1, gate * wide : (gate + 1) * wide] = parts[part][
                gate : gate + 1
            ]
    at = lax.broadcasted_iota(jnp.int32, (total, 4 * wide), 0)
    gate = lax.broadcasted_iota(jnp.int32, (1, 4 * wide), 1) // wide
    match = at == tables[0:1, :].astype(jnp.int32) * 4 + gate
    pickers = [
        jnp.where(match, tables[part : part + 1, :], 0.0).astype(bf16) for part in range(1, 4)
    ]
    dims = (((0,), (0,)), ((), ()))
    for side in range(2):
        block = rows[:, side * span : side * span + cols]
        value = sum(lax.dot_general(p, block, dims, preferred_element_type=f32) for p in pickers)
        held[:, :, side * cols : (side + 1) * cols] = value.astype(bf16).reshape(
            held.shape[0], slots, cols
        )
    for out, step in zip(outs, STEPS):
        expert = lax.rem(zhi + step, 4)
        for gate_at in range(4):
            out[gate_at * slots : (gate_at + 1) * slots, :] = held[gate_at * 4 + expert]


def arrange(place, w_own, w_sib, blocks):
    core, zlo, xhi = place[1], place[2], place[3]
    size, cols = blocks.shape[1], w_own.shape[1]
    own_at = pl.multiple_of(core * cols, 128)
    sib_at = pl.multiple_of((1 - core) * cols, 128)
    for index in range(4):
        z = 1 - zlo if index < 2 else zlo
        x = 1 - xhi if index % 2 == 0 else xhi
        rows = pl.ds(pl.multiple_of((z * 2 + x) * size, size), size)
        blocks[index, :, pl.ds(own_at, cols)] = w_own[rows, :]
        blocks[index, :, pl.ds(sib_at, cols)] = w_sib[rows, :]


def products(which, first, second, blocks, out):
    size = blocks.shape[1]
    both = jnp.concatenate([first[...], second[...]], 0)
    dims = (((1,), (1,)), ((), ()))
    for index, block in enumerate(which):
        value = lax.dot_general(both, blocks[block], dims, preferred_element_type=jnp.float32)
        out[:, index * size : (index + 1) * size] = value.astype(out.dtype)


def finish(place, keep, got, gate_factor, up_factor, grad_gate, grad_up):
    zhi, core = place[0], place[1]
    for piece, step in enumerate(STEPS):
        at = lax.rem(zhi + 4 - step, 4)
        for rows, whose in ((keep, core), (got, 1 - core)):
            value = rows[piece]
            grad_gate[at, :, whose] = (value * gate_factor[at, :, whose]).astype(grad_gate.dtype)
            grad_up[at, :, whose] = (value * up_factor[at, :, whose]).astype(grad_up.dtype)


def on_device(grad_out, cross_rows, slot_rows, route_prob, w_down, gate_pre, up_pre):
    bf16, f32 = jnp.bfloat16, jnp.float32
    groups = cross_rows.shape[2]
    experts, slots = slot_rows.shape[2:]
    hidden, cols = w_down.shape[2:]
    block = gate_pre.shape[-1]
    zhi, zlo = lax.axis_index("zhi"), lax.axis_index("zlo")
    xhi, core = lax.axis_index("xhi"), lax.axis_index("core")
    node = lax.axis_index("y") * EXTENTS[1] + lax.axis_index("xlo")
    w_own = w_down[0, 0]

    behind = 2 * experts * slots
    span = cols + behind
    inputs = (cross_rows.reshape(1, groups), slot_rows[0, 0], route_prob[0, 0], grad_out)
    outgoing = pl.pallas_call(
        pack,
        out_shape=jax.ShapeDtypeStruct((groups, 4, 2, span), bf16),
        in_specs=[pl.BlockSpec(memory_space=pl.ANY)] * 4,
        out_specs=pl.BlockSpec(memory_space=pl.ANY),
        scratch_shapes=[pltpu.VMEM(v.shape, v.dtype) for v in inputs]
        + [
            pltpu.SemaphoreType.DMA((4,)),
            pltpu.VMEM((4, groups, 2, span), bf16),
            pltpu.SemaphoreType.DMA((4,)),
        ],
        compiler_params=pltpu.CompilerParams(vmem_limit_bytes=56 << 20),
    )(*inputs)
    outgoing = outgoing.reshape(groups * 4, 2, span)
    place = jnp.stack([zhi, core, zlo, xhi, node]).astype(jnp.int32)
    received = lax.all_to_all(
        outgoing,
        ("y", "xlo", "zlo", "xhi"),
        split_axis=0,
        concat_axis=0,
        tiled=True,
    ).reshape(groups * 4, 2 * span)

    w_sib = lax.ppermute(w_own, "core", SWAP)
    size = (4 * slots, 2 * cols)
    chosen = pl.pallas_call(
        choose,
        out_shape=[jax.ShapeDtypeStruct(size, bf16)] * 4,
        in_specs=[SMEM, VMEM],
        out_specs=[VMEM] * 4,
        scratch_shapes=[
            pltpu.VMEM((4 * experts, slots, 2 * cols), bf16),
            pltpu.VMEM((4, 4 * experts * slots), f32),
        ],
        compiler_params=pltpu.CompilerParams(vmem_limit_bytes=12 << 20),
        cost_estimate=pl.CostEstimate(flops=20 << 30, bytes_accessed=2 << 20, transcendentals=0),
    )(place, received)
    pieces = [chosen[0]]
    for step, out in zip(STEPS[1:], chosen[1:]):
        pairs = [(i, (i + step) % 4) for i in range(4)]
        pieces.append(lax.ppermute(out, "zhi", pairs))
    rows = 2 * size[0]
    half, quarter = hidden // 2, hidden // 4

    blocks = pl.pallas_call(
        arrange,
        out_shape=jax.ShapeDtypeStruct((4, quarter, 2 * cols), bf16),
        in_specs=[SMEM] + [VMEM] * 2,
        out_specs=VMEM,
        compiler_params=pltpu.CompilerParams(vmem_limit_bytes=12 << 20),
    )(place, w_own, w_sib)

    def multiply(first, second, which, kind):
        return pl.pallas_call(
            lambda *refs: products(which, *refs),
            out_shape=jax.ShapeDtypeStruct((rows, half), kind),
            in_specs=[VMEM] * 3,
            out_specs=VMEM,
            compiler_params=pltpu.CompilerParams(vmem_limit_bytes=12 << 20),
            cost_estimate=pl.CostEstimate(
                flops=2 * rows * half * 2 * cols, bytes_accessed=3 << 20, transcendentals=0
            ),
        )(first, second, blocks)

    give_a = multiply(pieces[0], pieces[1], (0, 2), bf16)
    got_a = lax.ppermute(give_a, "xhi", SWAP)
    third, fourth, give_a = lax.optimization_barrier((pieces[2], pieces[3], give_a))
    give_b = multiply(third, fourth, (0, 1), bf16)
    first, give_b = lax.optimization_barrier((pieces[0], give_b))
    keep_a = multiply(first, pieces[1], (1, 3), f32)
    got_b = lax.ppermute(give_b, "zlo", SWAP)
    give_a = (keep_a[:, :quarter] + got_a[:, :quarter].astype(f32)).astype(bf16)
    keep_a = keep_a[:, quarter:] + got_a[:, quarter:].astype(f32)
    third, give_a = lax.optimization_barrier((third, give_a))
    got_a = lax.ppermute(give_a, "zlo", SWAP)
    keep_b = multiply(third, fourth, (2, 3), f32)
    give_b = (keep_b[:, :quarter] + got_b[:, :quarter].astype(f32)).astype(bf16)
    keep_b = keep_b[:, quarter:] + got_b[:, quarter:].astype(f32)
    got_b = lax.ppermute(give_b, "xhi", SWAP)
    total = jnp.concatenate([keep_a + got_a.astype(f32), keep_b + got_b.astype(f32)], 0)
    give = lax.dynamic_slice_in_dim(total, (1 - core) * block, block, 1)
    keep = lax.dynamic_slice_in_dim(total, core * block, block, 1)
    got = lax.ppermute(give, "core", SWAP)

    gate_vals = gate_pre.astype(f32)
    up_vals = up_pre.astype(f32)
    sigma = jax.nn.sigmoid(gate_vals)
    up_factor = gate_vals * sigma
    gate_factor = up_vals * sigma * (1.0 + gate_vals * (1.0 - sigma))
    deep = (4, 4, 2, slots, block)
    part = (4, 4, slots, block)
    grad_gate, grad_up = pl.pallas_call(
        finish,
        out_shape=[jax.ShapeDtypeStruct(deep, bf16)] * 2,
        in_specs=[SMEM] + [VMEM] * 4,
        out_specs=[VMEM] * 2,
        compiler_params=pltpu.CompilerParams(vmem_limit_bytes=8 << 20),
    )(
        place,
        keep.reshape(part),
        got.reshape(part),
        gate_factor.reshape(deep),
        up_factor.reshape(deep),
    )
    return grad_gate.reshape(gate_pre.shape), grad_up.reshape(up_pre.shape)


def solution(mesh):
    fine = Mesh(mesh.devices.reshape(EXTENTS), NAMES)
    node, expert = NAMES[:2], NAMES[2:]
    flat = P(node, expert, None, None)
    deep = P(node, expert, None, None, None)
    return jax.shard_map(
        on_device,
        mesh=fine,
        in_specs=(P(node + expert, None), flat, flat, flat, flat, deep, deep),
        out_specs=(deep, deep),
        check_vma=False,
    )
```

```python
import jax
import jax.numpy as jnp
from jax import lax
from jax.experimental import pallas as pl
from jax.experimental.pallas import tpu as pltpu
from jax.sharding import Mesh, PartitionSpec as P

NAMES = ("y", "xlo", "zhi", "zlo", "xhi", "core")
EXTENTS = (8, 4, 4, 2, 2, 2)
SWAP = ((0, 1), (1, 0))
STEPS = (0, 1, 2, 3)
SMEM = pl.BlockSpec(memory_space=pltpu.SMEM)
VMEM = pl.BlockSpec(memory_space=pltpu.VMEM)


def pack(crossing_in, slots_in, weights_in, tokens_in, packed, *held):
    arrivals, built, leaving = held[4:]
    sources = (crossing_in, slots_in, weights_in, tokens_in)
    copies = [
        pltpu.make_async_copy(source, held[index], arrivals.at[index])
        for index, source in enumerate(sources)
    ]
    for copy in copies[::-1]:
        copy.start()
    for copy in copies[:3]:
        copy.wait()
    crossing, slot_rows, weights, tokens = held[:4]
    f32, bf16 = jnp.float32, jnp.bfloat16
    count, cols = tokens.shape[0], tokens.shape[1] // 8
    groups, span = crossing.shape[1], packed.shape[3]
    weight = weights[...]
    high = weight.astype(bf16).astype(f32)
    middle = (weight - high).astype(bf16).astype(f32)
    low = weight - high - middle
    parts = jnp.concatenate([slot_rows[...].astype(f32), high, middle, low], 0).astype(bf16)
    lines, slots = parts.shape
    behind = span - cols
    spread = (
        lax.broadcasted_iota(jnp.int32, (slots, behind), 1) % slots
        == lax.broadcasted_iota(jnp.int32, (slots, behind), 0)
    ).astype(bf16)
    spread = jnp.dot(parts, spread, preferred_element_type=f32)
    line = lax.broadcasted_iota(jnp.int32, (lines, behind), 0)
    place = lax.broadcasted_iota(jnp.int32, (lines, behind), 1) // slots
    table = [
        jnp.sum(
            jnp.where(line == place + side * lines // 2, spread, 0.0), axis=0, keepdims=True
        ).astype(bf16)
        for side in range(2)
    ]
    half = lax.broadcasted_iota(jnp.int32, (groups, 2 * groups), 1) // 2
    twice = (half == lax.broadcasted_iota(jnp.int32, (groups, 2 * groups), 0)).astype(bf16)
    token = jnp.dot(crossing[...].astype(bf16), twice, preferred_element_type=f32)
    side = lax.broadcasted_iota(jnp.int32, (1, 2 * groups), 1) % 2
    at = lax.broadcasted_iota(jnp.int32, (2 * count, 2 * groups), 0)
    picker = (at == side * count + token.astype(jnp.int32)).astype(bf16)
    odd = lax.broadcasted_iota(jnp.int32, (2 * groups, behind), 0) % 2 == 1
    tail = jnp.where(odd, table[1].astype(f32), table[0].astype(f32)).astype(bf16)
    copies[3].wait()
    out_copies = []
    for pair in range(4):
        start = 2 * pair * cols
        both = jnp.concatenate(
            [tokens[:, start : start + cols], tokens[:, start + cols : start + 2 * cols]], 0
        )
        value = lax.dot_general(
            picker, both, (((0,), (0,)), ((), ())), preferred_element_type=f32
        )
        rows = jnp.concatenate([value.astype(bf16), tail], 1)
        built[pair] = rows.reshape(groups, 2, cols + behind)
        copy = pltpu.make_async_copy(built.at[pair], packed.at[:, pair], leaving.at[pair])
        copy.start()
        out_copies.append(copy)
    for copy in out_copies:
        copy.wait()


def choose(place, rows, *outs_and_scratch):
    outs, (held, tables) = outs_and_scratch[:4], outs_and_scratch[4:]
    zhi, node = place[0], place[4]
    total, span = rows.shape[0], rows.shape[1] // 2
    cols = outs[0].shape[1] // 2
    slots = held.shape[1]
    wide = 4 * slots
    f32, bf16 = jnp.float32, jnp.bfloat16
    lane = lax.broadcasted_iota(jnp.int32, (8, total), 1)
    line = lax.broadcasted_iota(jnp.int32, (8, total), 0)
    own = (lane == node * 4 + line).astype(bf16)
    first = jnp.dot(own, rows[:, cols:span], preferred_element_type=f32)
    second = jnp.dot(own, rows[:, span + cols :], preferred_element_type=f32)
    parts = (first[:, :wide], first[:, wide:], second[:, :wide], second[:, wide:])
    for gate in range(4):
        for part in range(4):
            tables[part : part + 1, gate * wide : (gate + 1) * wide] = parts[part][
                gate : gate + 1
            ]
    at = lax.broadcasted_iota(jnp.int32, (total, 4 * wide), 0)
    gate = lax.broadcasted_iota(jnp.int32, (1, 4 * wide), 1) // wide
    match = at == tables[0:1, :].astype(jnp.int32) * 4 + gate
    pickers = [
        jnp.where(match, tables[part : part + 1, :], 0.0).astype(bf16) for part in range(1, 4)
    ]
    dims = (((0,), (0,)), ((), ()))
    for side in range(2):
        block = rows[:, side * span : side * span + cols]
        value = sum(lax.dot_general(p, block, dims, preferred_element_type=f32) for p in pickers)
        held[:, :, side * cols : (side + 1) * cols] = value.astype(bf16).reshape(
            held.shape[0], slots, cols
        )
    for out, step in zip(outs, STEPS):
        expert = lax.rem(zhi + step, 4)
        for gate_at in range(4):
            out[gate_at * slots : (gate_at + 1) * slots, :] = held[gate_at * 4 + expert]


def arrange(place, w_own, w_sib, blocks):
    core, zlo, xhi = place[1], place[2], place[3]
    size, cols = blocks.shape[1], w_own.shape[1]
    own_at = pl.multiple_of(core * cols, 128)
    sib_at = pl.multiple_of((1 - core) * cols, 128)
    for index in range(4):
        z = 1 - zlo if index < 2 else zlo
        x = 1 - xhi if index % 2 == 0 else xhi
        rows = pl.ds(pl.multiple_of((z * 2 + x) * size, size), size)
        blocks[index, :, pl.ds(own_at, cols)] = w_own[rows, :]
        blocks[index, :, pl.ds(sib_at, cols)] = w_sib[rows, :]


def products(which, first, second, blocks, out):
    size = blocks.shape[1]
    both = jnp.concatenate([first[...], second[...]], 0)
    dims = (((1,), (1,)), ((), ()))
    for index, block in enumerate(which):
        value = lax.dot_general(both, blocks[block], dims, preferred_element_type=jnp.float32)
        out[:, index * size : (index + 1) * size] = value.astype(out.dtype)


def finish(place, keep, got, gate_factor, up_factor, grad_gate, grad_up):
    zhi, core = place[0], place[1]
    for piece, step in enumerate(STEPS):
        at = lax.rem(zhi + 4 - step, 4)
        for rows, whose in ((keep, core), (got, 1 - core)):
            value = rows[piece]
            grad_gate[at, :, whose] = (value * gate_factor[at, :, whose]).astype(grad_gate.dtype)
            grad_up[at, :, whose] = (value * up_factor[at, :, whose]).astype(grad_up.dtype)


def on_device(grad_out, cross_rows, slot_rows, route_prob, w_down, gate_pre, up_pre):
    bf16, f32 = jnp.bfloat16, jnp.float32
    groups = cross_rows.shape[2]
    experts, slots = slot_rows.shape[2:]
    hidden, cols = w_down.shape[2:]
    block = gate_pre.shape[-1]
    zhi, zlo = lax.axis_index("zhi"), lax.axis_index("zlo")
    xhi, core = lax.axis_index("xhi"), lax.axis_index("core")
    node = lax.axis_index("y") * EXTENTS[1] + lax.axis_index("xlo")
    w_own = w_down[0, 0]

    behind = 2 * experts * slots
    span = cols + behind
    inputs = (cross_rows.reshape(1, groups), slot_rows[0, 0], route_prob[0, 0], grad_out)
    outgoing = pl.pallas_call(
        pack,
        out_shape=jax.ShapeDtypeStruct((groups, 4, 2, span), bf16),
        in_specs=[pl.BlockSpec(memory_space=pl.ANY)] * 4,
        out_specs=pl.BlockSpec(memory_space=pl.ANY),
        scratch_shapes=[pltpu.VMEM(v.shape, v.dtype) for v in inputs]
        + [
            pltpu.SemaphoreType.DMA((4,)),
            pltpu.VMEM((4, groups, 2, span), bf16),
            pltpu.SemaphoreType.DMA((4,)),
        ],
        compiler_params=pltpu.CompilerParams(vmem_limit_bytes=56 << 20),
    )(*inputs)
    outgoing = outgoing.reshape(groups * 4, 2, span)
    place = jnp.stack([zhi, core, zlo, xhi, node]).astype(jnp.int32)
    received = lax.all_to_all(
        outgoing,
        ("y", "xlo", "zlo", "xhi"),
        split_axis=0,
        concat_axis=0,
        tiled=True,
    ).reshape(groups * 4, 2 * span)

    w_sib = lax.ppermute(w_own, "core", SWAP)
    size = (4 * slots, 2 * cols)
    chosen = pl.pallas_call(
        choose,
        out_shape=[jax.ShapeDtypeStruct(size, bf16)] * 4,
        in_specs=[SMEM, VMEM],
        out_specs=[VMEM] * 4,
        scratch_shapes=[
            pltpu.VMEM((4 * experts, slots, 2 * cols), bf16),
            pltpu.VMEM((4, 4 * experts * slots), f32),
        ],
        compiler_params=pltpu.CompilerParams(vmem_limit_bytes=12 << 20),
        cost_estimate=pl.CostEstimate(flops=20 << 30, bytes_accessed=2 << 20, transcendentals=0),
    )(place, received)
    pieces = [chosen[0]]
    for step, out in zip(STEPS[1:], chosen[1:]):
        pairs = [(i, (i + step) % 4) for i in range(4)]
        pieces.append(lax.ppermute(out, "zhi", pairs))
    rows = 2 * size[0]
    half, quarter = hidden // 2, hidden // 4

    blocks = pl.pallas_call(
        arrange,
        out_shape=jax.ShapeDtypeStruct((4, quarter, 2 * cols), bf16),
        in_specs=[SMEM] + [VMEM] * 2,
        out_specs=VMEM,
        compiler_params=pltpu.CompilerParams(vmem_limit_bytes=12 << 20),
    )(place, w_own, w_sib)

    def multiply(first, second, which, kind):
        return pl.pallas_call(
            lambda *refs: products(which, *refs),
            out_shape=jax.ShapeDtypeStruct((rows, half), kind),
            in_specs=[VMEM] * 3,
            out_specs=VMEM,
            compiler_params=pltpu.CompilerParams(vmem_limit_bytes=12 << 20),
            cost_estimate=pl.CostEstimate(
                flops=2 * rows * half * 2 * cols, bytes_accessed=3 << 20, transcendentals=0
            ),
        )(first, second, blocks)

    give_a = multiply(pieces[0], pieces[1], (0, 2), bf16)
    got_a = lax.ppermute(give_a, "xhi", SWAP)
    third, fourth, give_a = lax.optimization_barrier((pieces[2], pieces[3], give_a))
    give_b = multiply(third, fourth, (0, 1), bf16)
    first, give_b = lax.optimization_barrier((pieces[0], give_b))
    keep_a = multiply(first, pieces[1], (1, 3), f32)
    got_b = lax.ppermute(give_b, "zlo", SWAP)
    give_a = (keep_a[:, :quarter] + got_a[:, :quarter].astype(f32)).astype(bf16)
    keep_a = keep_a[:, quarter:] + got_a[:, quarter:].astype(f32)
    third, give_a = lax.optimization_barrier((third, give_a))
    got_a = lax.ppermute(give_a, "zlo", SWAP)
    keep_b = multiply(third, fourth, (2, 3), f32)
    give_b = (keep_b[:, :quarter] + got_b[:, :quarter].astype(f32)).astype(bf16)
    keep_b = keep_b[:, quarter:] + got_b[:, quarter:].astype(f32)
    got_b = lax.ppermute(give_b, "xhi", SWAP)
    total = jnp.concatenate([keep_a + got_a.astype(f32), keep_b + got_b.astype(f32)], 0)
    give = lax.dynamic_slice_in_dim(total, (1 - core) * block, block, 1)
    keep = lax.dynamic_slice_in_dim(total, core * block, block, 1)
    got = lax.ppermute(give, "core", SWAP)

    gate_vals = gate_pre.astype(f32)
    up_vals = up_pre.astype(f32)
    sigma = jax.nn.sigmoid(gate_vals)
    up_factor = gate_vals * sigma
    gate_factor = up_vals * sigma * (1.0 + gate_vals * (1.0 - sigma))
    deep = (4, 4, 2, slots, block)
    part = (4, 4, slots, block)
    grad_gate, grad_up = pl.pallas_call(
        finish,
        out_shape=[jax.ShapeDtypeStruct(deep, bf16)] * 2,
        in_specs=[SMEM] + [VMEM] * 4,
        out_specs=[VMEM] * 2,
        compiler_params=pltpu.CompilerParams(vmem_limit_bytes=8 << 20),
    )(
        place,
        keep.reshape(part),
        got.reshape(part),
        gate_factor.reshape(deep),
        up_factor.reshape(deep),
    )
    return grad_gate.reshape(gate_pre.shape), grad_up.reshape(up_pre.shape)


def solution(mesh):
    fine = Mesh(mesh.devices.reshape(EXTENTS), NAMES)
    node, expert = NAMES[:2], NAMES[2:]
    flat = P(node, expert, None, None)
    deep = P(node, expert, None, None, None)
    return jax.shard_map(
        on_device,
        mesh=fine,
        in_specs=(P(node + expert, None), flat, flat, flat, flat, deep, deep),
        out_specs=(deep, deep),
        check_vma=False,
    )
```
